32 devices in a mesh: replica: 8 (over z, y), fsdp: 4 (over x, core).
Axes of the slice: x: 2, y: 2, z: 4, core: 2. Of those that a mesh axis runs over, the one named last changes fastest.
Arguments:
- hidden_in: bfloat16 [32, 1024, 1024], P(('replica', 'fsdp')), may hold values from -6 to 6
- out_grad: bfloat16 [32, 1024, 1024], P(('replica', 'fsdp')), may hold values from -6 to 6
- norm1_gain: bfloat16 [1024], P('fsdp'), may hold values from 0.5 to 1.5
- in_weight: bfloat16 [1024, 3328], P('fsdp'), may hold values from -0.1875 to 0.1875
- step_weight: bfloat16 [1024, 24], P('fsdp'), may hold values from -0.1875 to 0.1875
- conv_weight: bfloat16 [1792, 4], P('fsdp'), may hold values from -3 to 3
- conv_bias: bfloat16 [1792], P('fsdp'), may hold values from -1.5 to 1.5
- step_bias: bfloat16 [24], P('fsdp'), may hold values from -6 to -2
- decay_log: bfloat16 [24], P('fsdp'), may hold values from 0 to 2.765625
- skip_gain: bfloat16 [24], P('fsdp'), may hold values from 0.5 to 1.5
- ssm_gain: bfloat16 [1536], P('fsdp'), may hold values from 0.5 to 1.5
- mamba_out_weight: bfloat16 [1536, 1024], P('fsdp'), may hold values from -0.15625 to 0.15625
- query_weight: bfloat16 [1024, 512], P('fsdp'), may hold values from -0.1875 to 0.1875
- key_value_weight: bfloat16 [1024, 256], P('fsdp'), may hold values from -0.1875 to 0.1875
- attention_out_weight: bfloat16 [512, 1024], P('fsdp'), may hold values from -2 to 2
- norm2_gain: bfloat16 [1024], P('fsdp'), may hold values from 0.5 to 1.5
- gate_weight: bfloat16 [1024, 2048], P('fsdp'), may hold values from -0.1875 to 0.1875
- up_weight: bfloat16 [1024, 2048], P('fsdp'), may hold values from -0.1875 to 0.1875
- down_weight: bfloat16 [2048, 1024], P('fsdp'), may hold values from -0.125 to 0.125
Outputs:
- hidden_out: bfloat16 [32, 1024, 1024], P(('replica', 'fsdp'))
- input_grad: float32 [32, 1024, 1024], P(('replica', 'fsdp'))
- grad_norm1_gain: float32 [1024], P('fsdp')
- grad_in_weight: float32 [1024, 3328], P('fsdp')
- grad_step_weight: float32 [1024, 24], P('fsdp')
- grad_conv_weight: float32 [1792, 4], P('fsdp')
- grad_conv_bias: float32 [1792], P('fsdp')
- grad_step_bias: float32 [24], P('fsdp')
- grad_decay_log: float32 [24], P('fsdp')
- grad_skip_gain: float32 [24], P('fsdp')
- grad_ssm_gain: float32 [1536], P('fsdp')
- grad_mamba_out_weight: float32 [1536, 1024], P('fsdp')
- grad_query_weight: float32 [1024, 512], P('fsdp')
- grad_key_value_weight: float32 [1024, 256], P('fsdp')
- grad_attention_out_weight: float32 [512, 1024], P('fsdp')
- grad_norm2_gain: float32 [1024], P('fsdp')
- grad_gate_weight: float32 [1024, 2048], P('fsdp')
- grad_up_weight: float32 [1024, 2048], P('fsdp')
- grad_down_weight: float32 [2048, 1024], P('fsdp')
The draws below stay inside these ranges and needn't reach their ends.
All inputs are finite; a program needn't handle non-finite values.
Results may differ from the reference program's by a relative error of at most 0.013.
Values may be sent and summed in bfloat16 or wider, within the bound.
A program may use at most 384 MiB of HBM per device.

```python
import math
import jax
import jax.numpy as jnp
from jax import lax

D = 1024
MHEADS = 24
MHEAD_DIM = 64
STATE = 128
CONV = 4
AHEADS = 8
KVHEADS = 2
HEAD_DIM = 64
FF = 2048
LEN = 1024
SEQS = 32
DSSM = 1536
XBC = 1792
QDIM = 512
KVDIM = 128
QBLK = 512
SBLK = 256


def steps_of(stream_key, dims, cuts, smallest, largest):
    def one(position, shards_of):
        draws = jax.random.uniform(jax.random.fold_in(jax.random.fold_in(stream_key, 6), position), (shards_of,), jnp.float32, smallest / len(cuts), largest / len(cuts))
        return jnp.repeat(jnp.exp(draws), dims[position] // shards_of).reshape((-1,) + (1,) * (len(dims) - position - 1))

    level = one(*cuts[0])
    for cut in cuts[1:]:
        level = level * one(*cut)
    return level


def normal_values(key, extent, scale, limit, cuts=(), kind=jnp.bfloat16):
    array = jax.random.normal(key, extent, jnp.float32) * scale
    if len(cuts) > 0:
        array = steps_of(key, extent, cuts, -0.22, 0.18) * array
    return jnp.clip(array, min=-limit, max=limit).astype(kind)


def setup_inputs(seed: int = 0) -> dict:
    streams_of = jax.random.split(jax.random.key(seed), 20)
    hidden_in = normal_values(streams_of[0], (SEQS, LEN, D), 1.0, 6.0, ((0, 32),))
    out_grad = normal_values(streams_of[1], (SEQS, LEN, D), 1.0, 6.0, ((0, 32),))
    norm1_gain = jnp.clip(1.0 + 0.1 * jax.random.normal(streams_of[2], (D,), jnp.float32), 0.5, 1.5).astype(jnp.bfloat16)
    in_weight = normal_values(streams_of[3], (D, DSSM + XBC), D ** -0.5, 0.1875, ((0, 4),))
    step_weight = normal_values(streams_of[4], (D, MHEADS), D ** -0.5, 0.1875, ((0, 4),))
    conv_weight = normal_values(streams_of[5], (XBC, CONV), CONV ** -0.5, 3.0, ((0, 4),))
    conv_bias = normal_values(streams_of[6], (XBC,), 0.3, 1.5, ((0, 4),))
    step_bias = jnp.clip(-6.0 + 4.0 * jax.random.uniform(streams_of[7], (MHEADS,), jnp.float32) ** steps_of(streams_of[7], (MHEADS,), ((0, 4),), -0.2, 0.2), -6.0, -2.0).astype(jnp.bfloat16)
    decay_log = jnp.clip(2.765625 * jax.random.uniform(streams_of[8], (MHEADS,), jnp.float32) ** steps_of(streams_of[8], (MHEADS,), ((0, 4),), -0.2, 0.2), 0.0, 2.765625).astype(jnp.bfloat16)
    skip_gain = jnp.clip(0.5 + 1.0 * jax.random.uniform(streams_of[9], (MHEADS,), jnp.float32) ** steps_of(streams_of[9], (MHEADS,), ((0, 4),), -0.2, 0.2), 0.5, 1.5).astype(jnp.bfloat16)
    ssm_gain = jnp.clip(1.0 + 0.1 * jax.random.normal(streams_of[10], (DSSM,), jnp.float32), 0.5, 1.5).astype(jnp.bfloat16)
    mamba_out_weight = normal_values(streams_of[11], (DSSM, D), DSSM ** -0.5, 0.15625, ((0, 4),))
    query_weight = normal_values(streams_of[12], (D, QDIM), D ** -0.5, 0.1875, ((0, 4),))
    key_value_weight = normal_values(streams_of[13], (D, 2 * KVDIM), D ** -0.5, 0.1875, ((0, 4),))
    attention_out_weight = normal_values(streams_of[14], (QDIM, D), (max(1, QDIM // 64)) ** -0.5, 2.0, ((0, 4),))
    norm2_gain = jnp.clip(1.0 + 0.1 * jax.random.normal(streams_of[15], (D,), jnp.float32), 0.5, 1.5).astype(jnp.bfloat16)
    gate_weight = normal_values(streams_of[16], (D, FF), D ** -0.5, 0.1875, ((0, 4),))
    up_weight = normal_values(streams_of[17], (D, FF), D ** -0.5, 0.1875, ((0, 4),))
    down_weight = normal_values(streams_of[18], (FF, D), FF ** -0.5, 0.125, ((0, 4),))
    return {"hidden_in": hidden_in, "out_grad": out_grad, "norm1_gain": norm1_gain, "in_weight": in_weight, "step_weight": step_weight, "conv_weight": conv_weight, "conv_bias": conv_bias, "step_bias": step_bias, "decay_log": decay_log, "skip_gain": skip_gain, "ssm_gain": ssm_gain, "mamba_out_weight": mamba_out_weight, "query_weight": query_weight, "key_value_weight": key_value_weight, "attention_out_weight": attention_out_weight, "norm2_gain": norm2_gain, "gate_weight": gate_weight, "up_weight": up_weight, "down_weight": down_weight}


EPSILON = 1e-05
ROPE_BASE = 100000000000.0
PRECISE = lax.Precision.HIGHEST

@jax.custom_vjp
def low(v):
    return lax.optimization_barrier(v.astype(jnp.bfloat16)).astype(jnp.float32)

@jax.custom_vjp
def low_back(v):
    return v

def low_keep(v):
    return (low(v), None)

def low_pass(kept, grad):
    return (grad,)

def back_keep(v):
    return (v, None)

def back_low(kept, grad):
    return (low(grad),)
low.defvjp(low_keep, low_pass)
low_back.defvjp(back_keep, back_low)

def product(pattern, first_op, second_op):
    return jnp.einsum(pattern, first_op, second_op, precision=PRECISE)

def rms_norm(tensor, scale_gain):
    return tensor * lax.rsqrt(lax.optimization_barrier(jnp.mean(tensor * tensor, axis=-1, keepdims=True)) + EPSILON) * scale_gain

def rotate(tensor):
    length = tensor.shape[0]
    width = tensor.shape[-1]
    half_width = width // 2
    frequency = ROPE_BASE ** (-2.0 * jnp.arange(half_width, dtype=jnp.float32) / width)
    angles = jnp.arange(length, dtype=jnp.float32)[:, None] * frequency[None, :]
    target_shape = (length,) + (1,) * (tensor.ndim - 2) + (half_width,)
    cosine = jnp.cos(angles).reshape(target_shape)
    sines = jnp.sin(angles).reshape(target_shape)
    former = tensor[..., :half_width]
    latter = tensor[..., half_width:]
    return jnp.concatenate([former * cosine - latter * sines, latter * cosine + former * sines], axis=-1)

def attend(queries, key_heads, values):
    length = queries.shape[0]
    block_count = length // QBLK
    blocks = queries.reshape((block_count, QBLK) + queries.shape[1:])
    starts = jnp.arange(block_count) * QBLK
    positions = jnp.arange(length)

    def one_block(pieces):
        query_part, first_row = pieces
        scores = low_back(product('qkgd,skd->qkgs', query_part, key_heads) * (1.0 / math.sqrt(HEAD_DIM)))
        row_ids = first_row + jnp.arange(QBLK)
        allowed = positions[None, :] <= row_ids[:, None]
        scores = jnp.where(allowed[:, None, None, :], scores, -1e+30)
        highest = lax.optimization_barrier(jnp.max(scores, axis=-1, keepdims=True))
        weights = jnp.exp(scores - highest)
        weights = low(weights / lax.optimization_barrier(jnp.sum(weights, axis=-1, keepdims=True)))
        return product('qkgs,skd->qkgd', weights, values)
    output = lax.map(jax.checkpoint(one_block), (blocks, starts))
    return output.reshape(queries.shape)

def state_space(ssm_x, step_sizes, log_decay, entry_vec, readout_vec):
    length = ssm_x.shape[0]
    block_count = length // SBLK
    inputs = ssm_x.reshape(block_count, SBLK, MHEADS, MHEAD_DIM)
    steps = step_sizes.reshape(block_count, SBLK, MHEADS)
    running = jnp.cumsum(log_decay.reshape(block_count, SBLK, MHEADS), axis=1)
    entries = entry_vec.reshape(block_count, SBLK, STATE)
    readouts = readout_vec.reshape(block_count, SBLK, STATE)
    inner_ids = jnp.arange(SBLK)
    below_diag = inner_ids[:, None] >= inner_ids[None, :]
    spread = jnp.where(below_diag[None, :, :, None], running[:, :, None, :] - running[:, None, :, :], -1e+30)
    decay = jnp.exp(spread)
    matching = jnp.einsum('bin,bjn->bij', readouts, entries, precision=PRECISE)
    mixing = matching[..., None] * decay * steps[:, None, :, :]
    diagonal = jnp.einsum('bijh,bjhp->bihp', mixing, inputs, precision=PRECISE)
    tail = jnp.exp(running[:, -1:, :] - running) * steps
    local_states = jnp.einsum('bjh,bjhp,bjn->bhpn', tail, inputs, entries, precision=PRECISE)

    def carry_step(state, pieces):
        local_state, total = pieces
        return (jnp.exp(total)[:, None, None] * state + local_state, state)
    start_state = jnp.zeros((MHEADS, MHEAD_DIM, STATE), jnp.float32)
    _, entering = lax.scan(carry_step, start_state, (local_states, running[:, -1, :]))
    carried = jnp.einsum('bin,bhpn->bihp', readouts, entering, precision=PRECISE) * jnp.exp(running)[..., None]
    return (diagonal + carried).reshape(length, MHEADS, MHEAD_DIM)

def layer_forward(hidden, weights):
    norm1_gain, in_weight, step_weight, conv_weight, conv_bias, step_bias, decay_log, skip_gain, ssm_gain, mamba_out_weight, query_weight, key_value_weight, attention_out_weight, norm2_gain, gate_weight, up_weight, down_weight = weights
    length = hidden.shape[0]
    normed = low(rms_norm(hidden, norm1_gain))
    mixed_in = low_back(product('td,de->te', normed, in_weight))
    step_raw = low_back(product('td,de->te', normed, step_weight))
    gate_z = mixed_in[:, :DSSM]
    conv_in = mixed_in[:, DSSM:]
    padded = jnp.concatenate([jnp.zeros((CONV - 1, XBC), jnp.float32), conv_in], axis=0)
    conv_sum = conv_bias
    for offset in range(CONV):
        conv_sum = conv_sum + padded[offset:offset + length] * conv_weight[:, offset]
    conv_out = jax.nn.silu(conv_sum)
    ssm_x = conv_out[:, :DSSM].reshape(length, MHEADS, MHEAD_DIM)
    entry_vec = conv_out[:, DSSM:DSSM + STATE]
    readout_vec = conv_out[:, DSSM + STATE:]
    step_sizes = jax.nn.softplus(step_raw + step_bias)
    log_decay = -step_sizes * jnp.exp(decay_log)
    scanned = state_space(ssm_x, step_sizes, log_decay, entry_vec, readout_vec) + skip_gain[:, None] * ssm_x
    gated = scanned.reshape(length, DSSM) * jax.nn.silu(gate_z)
    mamba_branch = low_back(product('te,ed->td', low(rms_norm(gated, ssm_gain)), mamba_out_weight))
    queries = low_back(product('td,de->te', normed, query_weight))
    queries = queries.reshape(length, KVHEADS, AHEADS // KVHEADS, HEAD_DIM)
    key_value = low_back(product('td,de->te', normed, key_value_weight))
    key_heads = low(rotate(key_value[:, :KVDIM].reshape(length, KVHEADS, HEAD_DIM)))
    values = low(key_value[:, KVDIM:].reshape(length, KVHEADS, HEAD_DIM))
    queries = low(rotate(queries))
    attended = low(low_back(attend(queries, key_heads, values)))
    attn_branch = low_back(product('te,ed->td', attended.reshape(length, QDIM), attention_out_weight))
    middle = hidden + mamba_branch + attn_branch
    normed2 = low(rms_norm(middle, norm2_gain))
    gate_out = low_back(product('td,df->tf', normed2, gate_weight))
    up_out = low_back(product('td,df->tf', normed2, up_weight))
    activated = low(jax.nn.silu(gate_out) * up_out)
    return middle + low_back(product('tf,fd->td', activated, down_weight))

def reference(hidden_in, out_grad, norm1_gain, in_weight, step_weight, conv_weight, conv_bias, step_bias, decay_log, skip_gain, ssm_gain, mamba_out_weight, query_weight, key_value_weight, attention_out_weight, norm2_gain, gate_weight, up_weight, down_weight):
    weights = tuple((tensor.astype(jnp.float32) for tensor in (norm1_gain, in_weight, step_weight, conv_weight, conv_bias, step_bias, decay_log, skip_gain, ssm_gain, mamba_out_weight, query_weight, key_value_weight, attention_out_weight, norm2_gain, gate_weight, up_weight, down_weight)))

    def forward(hidden, params):

        def per_sequence(sequence):
            return layer_forward(sequence, params)
        return lax.map(jax.checkpoint(per_sequence), hidden)
    outputs, pullback = jax.vjp(forward, hidden_in.astype(jnp.float32), weights)
    input_grad, grads = pullback(out_grad.astype(jnp.float32))
    return (outputs.astype(jnp.bfloat16), input_grad, grads[0], grads[1], grads[2], grads[3], grads[4], grads[5], grads[6], grads[7], grads[8], grads[9], grads[10], grads[11], grads[12], grads[13], grads[14], grads[15], grads[16])
```

```python
import math

import jax
import jax.numpy as jnp
from jax import lax
from jax.sharding import PartitionSpec as P

MHEADS = 24
MHEAD_DIM = 64
STATE = 128
CONV = 4
AHEADS = 8
KVHEADS = 2
HEAD_DIM = 64
DSSM = 1536
XBC = 1792
QDIM = 512
KVDIM = 128
ABLK = 256
SBLK = 128


EPSILON = 1e-05
ROPE_BASE = 100000000000.0


def round_value(tensor):
    return lax.optimization_barrier(tensor.astype(jnp.bfloat16)).astype(jnp.float32)


def round_keep(tensor):
    return (round_value(tensor), None)


def round_pass(kept, grad):
    return (grad,)


def low(tensor):
    rounder = jax.custom_vjp(round_value)
    rounder.defvjp(round_keep, round_pass)
    return rounder(tensor)


def same_value(tensor):
    return tensor


def same_keep(tensor):
    return (tensor, None)


def grad_round(kept, grad):
    return (low(grad),)


def low_back(tensor):
    passer = jax.custom_vjp(same_value)
    passer.defvjp(same_keep, grad_round)
    return passer(tensor)


def pattern_parts(pattern):
    comma_at = [position for position, character in enumerate(pattern) if character == ","][0]
    arrow_at = [position for position, character in enumerate(pattern) if character == "-"][0]
    return (pattern[:comma_at], pattern[comma_at + 1 : arrow_at], pattern[arrow_at + 2 :])


def product_value(pattern, first_op, second_op):
    return jnp.einsum(
        pattern,
        first_op.astype(jnp.bfloat16),
        second_op.astype(jnp.bfloat16),
        preferred_element_type=jnp.float32,
    )


def product_keep(pattern, first_op, second_op):
    return (product_value(pattern, first_op, second_op), (first_op, second_op))


def product_back(pattern, saved_ops, cotangent):
    first_op, second_op = saved_ops
    left_form, right_form, target = pattern_parts(pattern)
    rounded = cotangent.astype(jnp.bfloat16)
    first_grad = jnp.einsum(
        target + "," + right_form + "->" + left_form,
        rounded,
        second_op.astype(jnp.bfloat16),
        preferred_element_type=jnp.float32,
    )
    second_grad = jnp.einsum(
        target + "," + left_form + "->" + right_form,
        rounded,
        first_op.astype(jnp.bfloat16),
        preferred_element_type=jnp.float32,
    )
    return (first_grad, second_grad)


def product(pattern, first_op, second_op):
    multiplier = jax.custom_vjp(product_value, nondiff_argnums=(0,))
    multiplier.defvjp(product_keep, product_back)
    return multiplier(pattern, first_op, second_op)


def rms_norm(tensor, scale_gain):
    return (
        tensor * lax.rsqrt(jnp.mean(tensor * tensor, axis=-1, keepdims=True) + EPSILON) * scale_gain
    )


def rotate(tensor):
    length = tensor.shape[0]
    width = tensor.shape[-1]
    half_width = width // 2
    frequency = ROPE_BASE ** (-2.0 * jnp.arange(half_width, dtype=jnp.float32) / width)
    angles = jnp.arange(length, dtype=jnp.float32)[:, None] * frequency[None, :]
    target_shape = (length,) + (1,) * (tensor.ndim - 2) + (half_width,)
    cosine = jnp.cos(angles).reshape(target_shape)
    sines = jnp.sin(angles).reshape(target_shape)
    former = tensor[..., :half_width]
    latter = tensor[..., half_width:]
    return jnp.concatenate(
        [former * cosine - latter * sines, latter * cosine + former * sines], axis=-1
    )


def attend_value(first_row, queries, keys, values):
    scores = product_value("kgqd,ksd->kgqs", queries, keys) * (1.0 / math.sqrt(HEAD_DIM))
    rows, columns = scores.shape[2:]
    allowed = jnp.arange(columns)[None, :] <= first_row + jnp.arange(rows)[:, None]
    scores = jnp.where(allowed, scores, -1e30)
    weights = jnp.exp(scores - jnp.max(scores, axis=-1, keepdims=True))
    probs = (weights / jnp.sum(weights, axis=-1, keepdims=True)).astype(jnp.bfloat16)
    return product_value("kgqs,ksd->kgqd", probs, values), probs


def attend_block(first_row, queries, keys, values):
    return attend_value(first_row, queries, keys, values)[0]


def attend_keep(first_row, queries, keys, values):
    output, probs = attend_value(first_row, queries, keys, values)
    return output, (queries, keys, values, probs)


def attend_back(first_row, kept, grad):
    queries, keys, values, probs = kept
    grad = grad.astype(jnp.bfloat16)
    value_grad = product_value("kgqs,kgqd->ksd", probs, grad)
    prob_grad = product_value("kgqd,ksd->kgqs", grad, values)
    wide = probs.astype(jnp.float32)
    centre = jnp.sum(prob_grad * wide, axis=-1, keepdims=True)
    score_grad = (wide * (prob_grad - centre)).astype(jnp.bfloat16)
    scale = 1.0 / math.sqrt(HEAD_DIM)
    query_grad = product_value("kgqs,ksd->kgqd", score_grad, keys) * scale
    key_grad = product_value("kgqs,kgqd->ksd", score_grad, queries) * scale
    return (query_grad, key_grad, value_grad)


def attend(queries, key_heads, values):
    length = queries.shape[0]
    queries = jnp.transpose(queries, (1, 2, 0, 3))
    keys = jnp.transpose(key_heads, (1, 0, 2))
    values = jnp.transpose(values, (1, 0, 2))
    blocker = jax.custom_vjp(attend_block, nondiff_argnums=(0,))
    blocker.defvjp(attend_keep, attend_back)
    parts = []
    for start in range(0, length, ABLK):
        stop = start + ABLK
        parts.append(blocker(start, queries[:, :, start:stop], keys[:, :stop], values[:, :stop]))
    return jnp.transpose(jnp.concatenate(parts, axis=2), (2, 0, 1, 3))


def mix_diagonal(matching, running, inputs):
    size = matching.shape[-1]
    ids = jnp.arange(size)
    below_diag = ids[:, None] >= ids[None, :]
    spread = jnp.where(below_diag, running[..., :, None] - running[..., None, :], -1e30)
    mixing = matching[:, None] * jnp.exp(spread)
    return product("bhij,bhjp->bhip", mixing, inputs)


def state_space(ssm_x, step_sizes, log_decay, entry_vec, readout_vec):
    length = ssm_x.shape[0]
    count = length // SBLK
    scaled = (ssm_x * step_sizes[:, :, None]).reshape(count, SBLK, MHEADS, MHEAD_DIM)
    inputs = jnp.transpose(scaled, (0, 2, 1, 3))
    logs = jnp.transpose(log_decay.reshape(count, SBLK, MHEADS), (0, 2, 1))
    ids = jnp.arange(SBLK)
    upper = (ids[:, None] <= ids[None, :]).astype(jnp.float32)
    running = jnp.einsum("bhj,ji->bhi", logs, upper, precision=lax.Precision.HIGHEST)
    entries = entry_vec.reshape(count, SBLK, STATE)
    readouts = readout_vec.reshape(count, SBLK, STATE)
    matching = product("bin,bjn->bij", readouts, entries)
    diagonal = jax.checkpoint(mix_diagonal)(matching, running, inputs)
    tail = jnp.exp(running[..., -1:] - running)
    local_states = product("bhjp,bjn->bhpn", tail[..., None] * inputs, entries)
    totals = jnp.exp(running[..., -1])[..., None, None]
    state = jnp.zeros((MHEADS, MHEAD_DIM, STATE), jnp.float32)
    entering = []
    for index in range(count):
        entering.append(state)
        state = totals[index] * state + local_states[index]
    entering = jnp.stack(entering)
    carried = product("bin,bhpn->bhip", readouts, entering) * jnp.exp(running)[..., None]
    mixed = jnp.transpose(diagonal + carried, (0, 2, 1, 3))
    return mixed.reshape(length, MHEADS, MHEAD_DIM)


def layer_forward(hidden, weights):
    (
        norm1_gain,
        in_weight,
        step_weight,
        conv_weight,
        conv_bias,
        step_bias,
        decay_log,
        skip_gain,
        ssm_gain,
        mamba_out_weight,
        query_weight,
        key_value_weight,
        attention_out_weight,
        norm2_gain,
        gate_weight,
        up_weight,
        down_weight,
    ) = weights
    length = hidden.shape[0]
    normed = low(rms_norm(hidden, norm1_gain))
    mixed_in = low_back(product("td,de->te", normed, in_weight))
    step_raw = low_back(product("td,de->te", normed, step_weight))
    gate_z = mixed_in[:, :DSSM]
    conv_in = mixed_in[:, DSSM:]
    padded = jnp.concatenate([jnp.zeros((CONV - 1, XBC), jnp.float32), conv_in], axis=0)
    conv_sum = conv_bias
    for offset in range(CONV):
        conv_sum = conv_sum + padded[offset : offset + length] * conv_weight[:, offset]
    conv_out = jax.nn.silu(conv_sum)
    ssm_x = conv_out[:, :DSSM].reshape(length, MHEADS, MHEAD_DIM)
    entry_vec = conv_out[:, DSSM : DSSM + STATE]
    readout_vec = conv_out[:, DSSM + STATE :]
    step_sizes = jax.nn.softplus(step_raw + step_bias)
    log_decay = -step_sizes * jnp.exp(decay_log)
    scanned = (
        state_space(ssm_x, step_sizes, log_decay, entry_vec, readout_vec)
        + skip_gain[:, None] * ssm_x
    )
    gated = scanned.reshape(length, DSSM) * jax.nn.silu(gate_z)
    mamba_branch = low_back(product("te,ed->td", low(rms_norm(gated, ssm_gain)), mamba_out_weight))
    queries = low_back(product("td,de->te", normed, query_weight))
    queries = queries.reshape(length, KVHEADS, AHEADS // KVHEADS, HEAD_DIM)
    key_value = low_back(product("td,de->te", normed, key_value_weight))
    key_heads = low(rotate(key_value[:, :KVDIM].reshape(length, KVHEADS, HEAD_DIM)))
    values = low(key_value[:, KVDIM:].reshape(length, KVHEADS, HEAD_DIM))
    queries = low(rotate(queries))
    attended = low(low_back(attend(queries, key_heads, values)))
    attn_branch = low_back(
        product("te,ed->td", attended.reshape(length, QDIM), attention_out_weight)
    )
    middle = hidden + mamba_branch + attn_branch
    normed2 = low(rms_norm(middle, norm2_gain))
    gate_out = low_back(product("td,df->tf", normed2, gate_weight))
    up_out = low_back(product("td,df->tf", normed2, up_weight))
    activated = low(jax.nn.silu(gate_out) * up_out)
    return middle + low_back(product("tf,fd->td", activated, down_weight))


SMALL = (0, 2, 3, 4, 5, 6, 7, 8, 13)
LARGE = (1, 11, 10, 9, 12, 14, 15, 16)


def forward(hidden, params):
    return jnp.stack([layer_forward(hidden[i], params) for i in range(hidden.shape[0])])


def body(hidden_in, out_grad, *shards):
    group = lax.axis_size("fsdp")
    params = [None] * len(shards)
    packed = jnp.concatenate([shards[i].reshape(-1) for i in SMALL])
    packed = lax.all_gather(packed, "fsdp", axis=0, tiled=False)
    for i in LARGE:
        params[i] = lax.all_gather(shards[i], "fsdp", axis=0, tiled=True)
    offset = 0
    for i in SMALL:
        piece = packed[:, offset : offset + shards[i].size]
        params[i] = piece.reshape((group * shards[i].shape[0],) + shards[i].shape[1:])
        offset += shards[i].size
    params = tuple(tensor.astype(jnp.float32) for tensor in params)
    outputs, pullback = jax.vjp(forward, hidden_in.astype(jnp.float32), params)
    input_grad, grads = pullback(out_grad.astype(jnp.float32))
    totals = [None] * len(shards)
    previous = None
    for members in ((16,), (15, 14), (12, 11), (9, 10, 1)):
        parts = tuple(
            lax.psum_scatter(
                grads[i].astype(jnp.bfloat16), "fsdp", scatter_dimension=0, tiled=True
            )
            for i in members
        )
        if previous is not None:
            parts, previous = lax.optimization_barrier((parts, previous))
        previous = lax.psum(parts, "replica")
        for i, total in zip(members, previous):
            totals[i] = total.astype(jnp.float32)
    flat = jnp.concatenate([grads[i].reshape(group, -1) for i in SMALL], axis=1)
    flat = lax.psum(flat, ("replica", "fsdp"))
    flat = lax.dynamic_index_in_dim(flat, lax.axis_index("fsdp"), 0, keepdims=False)
    offset = 0
    for i in SMALL:
        totals[i] = flat[offset : offset + shards[i].size].reshape(shards[i].shape)
        offset += shards[i].size
    return (outputs.astype(jnp.bfloat16), input_grad, *totals)


def solution(mesh):
    in_specs = (
        P(("replica", "fsdp"), None, None),
        P(("replica", "fsdp"), None, None),
        P("fsdp"),
        P("fsdp", None),
        P("fsdp", None),
        P("fsdp", None),
        P("fsdp"),
        P("fsdp"),
        P("fsdp"),
        P("fsdp"),
        P("fsdp"),
        P("fsdp", None),
        P("fsdp", None),
        P("fsdp", None),
        P("fsdp", None),
        P("fsdp"),
        P("fsdp", None),
        P("fsdp", None),
        P("fsdp", None),
    )
    out_specs = (
        P(("replica", "fsdp"), None, None),
        P(("replica", "fsdp"), None, None),
        P("fsdp"),
        P("fsdp", None),
        P("fsdp", None),
        P("fsdp", None),
        P("fsdp"),
        P("fsdp"),
        P("fsdp"),
        P("fsdp"),
        P("fsdp"),
        P("fsdp", None),
        P("fsdp", None),
        P("fsdp", None),
        P("fsdp", None),
        P("fsdp"),
        P("fsdp", None),
        P("fsdp", None),
        P("fsdp", None),
    )
    return jax.shard_map(body, mesh=mesh, in_specs=in_specs, out_specs=out_specs, check_vma=False)
```
